32 devices in a mesh: dp: 16 (over z, y, x), block: 2 (over core).
Axes of the slice: x: 2, y: 2, z: 4, core: 2. Of those that a mesh axis runs over, the one named last changes fastest.
Arguments:
- tokens: bfloat16 [16, 256, 4096], P('dp', 'block'), may hold values from -6 to 6
- cotangent: bfloat16 [16, 256, 4096], P('dp', 'block'), may hold values from -6 to 6
- w_up: bfloat16 [2, 4096, 512], P('block'), may hold values from -0.09375 to 0.09375
- w_down: bfloat16 [2, 512, 4096], P('block'), may hold values from -0.25 to 0.25
- active: int32 [16, 2], replicated, may hold values from 0 to 1, as said below
- width: int32 [16], replicated, may hold values from 8 to 16
- counts: int32 [2], replicated, may hold values from 16 to 63
Outputs:
- mixed: bfloat16 [16, 256, 4096], P('dp', 'block')
- input_grad: bfloat16 [16, 256, 4096], P('dp', 'block')
- up_grad: float32 [2, 4096, 512], P('block', 'dp')
- down_grad: float32 [2, 512, 4096], P('block', None, 'dp')
The draws below stay inside these ranges and needn't reach their ends.
Inputs may be any that keep to these rules, and one draw needn't show every extreme that they name: `active`: 0 or 1; blocks differ in how many micro-batches use them. micro-batch i uses the first 256 * width[i] features.
All inputs are finite; a program needn't handle non-finite values.
Results may differ from the reference program's by a relative error of at most 0.019.
Values may be sent and summed in bfloat16 or wider, within the bound.
A program may use at most 128 MiB of HBM per device.

```python
import math
import jax
import jax.numpy as jnp
from jax import lax

D = 4096
UNITS = 512
BLK_DEV = 1
MB_ROWS = 256
NBLK = 2
NMB = 16
WSTEP = 256
N_DP = 16
N_BLOCK = 2


def draw_active(key, part):
    key_rates, key_values = jax.random.split(jax.random.fold_in(key, 7))
    use_rates = jax.random.randint(key_rates, (NBLK,), 1, 8)
    raw_draws = jax.random.randint(key_values, (NMB, NBLK), 0, 8)
    return (raw_draws < use_rates[None, :]).astype(jnp.int32)


def touch_ends(result, rng, low, high):
    dims = result.shape
    index_at = [jax.random.randint(jax.random.fold_in(rng, axis), (), 0, dims[axis]) for axis in range(len(dims))]
    result = result.at[tuple(index_at)].set(low)
    longest = dims.index(max(dims))
    index_at[longest] = (index_at[longest] + 1) % dims[longest]
    return result.at[tuple(index_at)].set(high)


def with_spikes(result, key, source, target, parts, factor):
    owner, partner = [(jnp.arange(result.shape[position]) // (result.shape[position] // parts)).reshape([-1 if axis == position else 1 for axis in range(result.ndim)]) for position in (source, target)]
    chosen = jax.random.permutation(key, parts)[partner]
    strong = (owner == chosen) | (owner == (partner + parts // 2) % parts)
    return jnp.where(strong, factor * result, result)


def block_scale(key, extent, cuts, low, largest):
    level = 1.0
    for position, blocks in cuts:
        draws = jax.random.uniform(jax.random.fold_in(jax.random.fold_in(key, 6), position), (blocks,), jnp.float32, low / len(cuts), largest / len(cuts))
        level = level * jnp.repeat(jnp.exp(draws), extent[position] // blocks).reshape((-1,) + (1,) * (len(extent) - 1 - position))
    return level


def centred(rng, extent, scale, reach, cuts=(), kind=jnp.bfloat16):
    drawn = jax.random.normal(rng, extent, jnp.float32) * scale
    if len(cuts) > 0:
        drawn = block_scale(rng, extent, cuts, -0.22, 0.18) * drawn
    return jnp.clip(drawn, min=-reach, max=reach).astype(kind)


def heavy_noise(own_key, dims, scale, bound, pieces, heavy, held_as=jnp.bfloat16):
    result = scale * jax.random.normal(own_key, dims, jnp.float32)
    if pieces:
        result = result * block_scale(own_key, dims, pieces, -0.22, 0.18)
    return jnp.clip(with_spikes(result, jax.random.fold_in(own_key, 3), *heavy), -bound, bound).astype(held_as)


def setup_inputs(seed: int = 0) -> dict:
    streams_of = jax.random.split(jax.random.key(seed), 8)
    tokens = heavy_noise(streams_of[0], (NMB, MB_ROWS, D), 1.0, 6.0, ((0, 16), (1, 2)), (0, 2, 16, 2.0))
    cotangent = centred(streams_of[1], (NMB, MB_ROWS, D), 1.0, 6.0, ((0, 16), (1, 2)))
    w_up = centred(streams_of[2], (NBLK, D, UNITS), D ** -0.5, 0.09375, ((0, 2),))
    w_down = centred(streams_of[3], (NBLK, UNITS, D), UNITS ** -0.5, 0.25, ((0, 2),))
    active = draw_active(jax.random.fold_in(streams_of[7], 71), 0)
    width = touch_ends(jax.random.randint(streams_of[5], (NMB,), 8, 17), jax.random.fold_in(streams_of[5], 1), 8, 16).astype(jnp.int32)
    counts = jax.random.randint(streams_of[6], (NBLK,), N_DP, 4 * N_DP).astype(jnp.int32)
    return dict(tokens=tokens, cotangent=cotangent, w_up=w_up, w_down=w_down, active=active, width=width, counts=counts)


GELU_C = math.sqrt(2.0 / math.pi)

def gelu_parts(pre_vals):
    tanh_val = jnp.tanh(GELU_C * (pre_vals + 0.044715 * pre_vals * pre_vals * pre_vals))
    gelu_value = 0.5 * pre_vals * (1.0 + tanh_val)
    gelu_slope = 0.5 * (1.0 + tanh_val) + 0.5 * pre_vals * (1.0 - tanh_val * tanh_val) * GELU_C * (1.0 + 3.0 * 0.044715 * pre_vals * pre_vals)
    return (gelu_value, gelu_slope)

def round_trip(values):
    return lax.optimization_barrier(values.astype(jnp.bfloat16)).astype(jnp.float32)

def group_round(terms):
    grouped = terms.reshape(N_BLOCK, BLK_DEV, MB_ROWS, D).sum(axis=1)
    return round_trip(grouped).sum(axis=0)

def reference(tokens, cotangent, w_up, w_down, active, width, counts):
    up_full = w_up.astype(jnp.float32)
    down_full = w_down.astype(jnp.float32)
    gate_all = active.astype(jnp.float32)
    scale_all = gate_all / counts.astype(jnp.float32)[None, :]
    feat_ids = jnp.arange(D, dtype=jnp.int32)

    def one_batch(carry, inputs):
        up_acc, down_acc = carry
        x_rows, dy_rows, gate_row, scale_row, width_step = inputs
        feat_mask = (feat_ids < WSTEP * width_step).astype(jnp.bfloat16)
        masked_x = x_rows * feat_mask
        masked_dy = dy_rows * feat_mask
        pre_act = jnp.einsum('rd,bdu->bru', masked_x.astype(jnp.float32), up_full)
        gelu_value, gelu_slope = gelu_parts(pre_act)
        hidden = gelu_value.astype(jnp.bfloat16)
        out_terms = jnp.einsum('bru,bud->brd', hidden.astype(jnp.float32), down_full) * gate_row[:, None, None]
        mixed = (x_rows.astype(jnp.float32) + feat_mask.astype(jnp.float32) * group_round(out_terms)).astype(jnp.bfloat16)
        back_proj = jnp.einsum('rd,bud->bru', masked_dy.astype(jnp.float32), down_full)
        grad_hidden = (back_proj * gelu_slope).astype(jnp.bfloat16)
        in_terms = jnp.einsum('bru,bdu->brd', grad_hidden.astype(jnp.float32), up_full) * gate_row[:, None, None]
        input_grad = (dy_rows.astype(jnp.float32) + feat_mask.astype(jnp.float32) * group_round(in_terms)).astype(jnp.bfloat16)
        down_term = round_trip(scale_row[:, None, None] * jnp.einsum('bru,rd->bud', hidden.astype(jnp.float32), masked_dy.astype(jnp.float32)))
        up_term = round_trip(scale_row[:, None, None] * jnp.einsum('rd,bru->bdu', masked_x.astype(jnp.float32), grad_hidden.astype(jnp.float32)))
        return ((up_acc + up_term, down_acc + down_term), (mixed, input_grad))
    init = (jnp.zeros((NBLK, D, UNITS), jnp.float32), jnp.zeros((NBLK, UNITS, D), jnp.float32))
    sums, rows_out = lax.scan(one_batch, init, (tokens, cotangent, gate_all, scale_all, width))
    return (rows_out[0], rows_out[1], sums[0], sums[1])
```

```python
import functools
import math

import jax
import jax.numpy as jnp
from jax import lax
from jax.experimental import pallas as pl
from jax.experimental.pallas import tpu as pltpu
from jax.sharding import PartitionSpec as P

GELU_C = math.sqrt(2.0 / math.pi)
GROUP = 4
BF16 = jnp.bfloat16
F32 = jnp.float32


def gelu_parts(v):
    t = jnp.tanh(GELU_C * (v + 0.044715 * v * v * v))
    value = 0.5 * v * (1.0 + t)
    slope = 0.5 * (1.0 + t) + 0.5 * v * (1.0 - t * t) * GELU_C * (1.0 + 3.0 * 0.044715 * v * v)
    return value, slope


def kernel(
    n_dp, n_blk,
    x_hbm, dy_hbm, wu_hbm, wd_hbm, active, width, counts,
    mixed_hbm, ing_hbm, up_hbm, down_hbm,
    x_raw, dy_raw, wu, wd, x_own, y_own, x_all, y_all, h_all, g_all, h_t, g_t, pre, slope,
    out_part, in_part, out_got, in_got, partial, z_send, z_got, mixed_v, ing_v, grad_v,
    loc, sib_s, sib_r, a2a_s, a2a_r, fwd_s, fwd_r, gat_s, gat_r, rel_s, rel_r, red_s, red_r, zs, zr,
):
    me = lax.axis_index("dp")
    blk = lax.axis_index("block")
    steps = n_dp // GROUP
    rows_own, feats = x_raw.shape
    units = wu.shape[1]
    rows = rows_own * n_blk
    half = rows // 2
    chunk = feats // n_dp
    hi = lax.div(me, GROUP)
    lo = lax.rem(me, GROUP)
    lx = lax.rem(lo, 2)
    ly = lax.div(lo, 2)

    def mate(o):
        px = 1 - lx if o & 1 else lx
        py = 1 - ly if o & 2 else ly
        return py * 2 + px

    def at(dp, b):
        return {"dp": dp, "block": b}

    mesh_id = pl.DeviceIdType.MESH
    mates = {o: mate(o) for o in range(1, GROUP)}
    mate_id = {o: at(hi * GROUP + mates[o], blk) for o in mates}
    sibs = {k: lax.rem(blk + k, n_blk) for k in range(1, n_blk)}
    sib_id = {k: at(me, sibs[k]) for k in sibs}
    side_id = (at(me + GROUP, blk), at(me - GROUP, blk))
    has_right = hi < steps - 1
    has_left = hi > 0
    mine = pl.ds(pl.multiple_of(blk * rows_own, rows_own), rows_own)

    loads = [
        pltpu.make_async_copy(s, d, loc.at[i])
        for i, (s, d) in enumerate(((x_hbm, x_raw), (dy_hbm, dy_raw), (wu_hbm, wu), (wd_hbm, wd)))
    ]
    for c in loads:
        c.start()

    barrier = pltpu.get_barrier_semaphore()
    for dev in list(mate_id.values()) + list(sib_id.values()):
        pl.semaphore_signal(barrier, inc=1, device_id=dev, device_id_type=mesh_id)

    @pl.when(has_right)
    def _():
        pl.semaphore_signal(barrier, inc=1, device_id=side_id[0], device_id_type=mesh_id)

    @pl.when(has_left)
    def _():
        pl.semaphore_signal(barrier, inc=1, device_id=side_id[1], device_id_type=mesh_id)

    pl.semaphore_wait(
        barrier,
        len(mate_id) + len(sib_id) + has_right.astype(jnp.int32) + has_left.astype(jnp.int32),
    )

    def remote(src, dst, s, r, dev):
        return pltpu.make_async_remote_copy(
            src_ref=src, dst_ref=dst, send_sem=s, recv_sem=r, device_id=dev, device_id_type=mesh_id
        )

    limit = feats // 16 * width[me]
    gate = active[me, blk].astype(F32)
    inv = 1.0 / counts[blk].astype(F32)

    def chunk_mask(start, size, kind):
        col = lax.broadcasted_iota(jnp.int32, (1, size), 1) + start
        return jnp.where(col < limit, 1.0, 0.0).astype(kind)

    def mask_into(raw, own):
        for l in range(GROUP):
            for h in range(steps):
                c = h * GROUP + l
                own[l, h, mine, :] = raw[:, c * chunk:(c + 1) * chunk] * chunk_mask(c * chunk, chunk, BF16)

    def share(t, own):
        out = []
        for k in sibs:
            cp = remote(own.at[:, :, mine, :], own.at[:, :, mine, :], sib_s.at[t, k], sib_r.at[t, k], sib_id[k])
            cp.start()
            out.append(cp)
        return out

    def spread(t, own, every):
        out = {}
        for o in mates:
            cp = remote(
                own.at[mates[o], :, mine, :], every.at[:, o, mine, :], a2a_s.at[t, o], a2a_r.at[t, o], mate_id[o]
            )
            cp.start()
            out[o] = cp
        return out

    def forward(t, every, copies):
        out = []
        for o in (1, 2, 3):
            copies[o].wait_recv()
            for k in sibs:
                cp = remote(
                    every.at[:, o, mine, :], every.at[:, o, mine, :], fwd_s.at[t, o, k], fwd_r.at[t, o, k], sib_id[k]
                )
                cp.start()
                out.append(cp)
        return out

    def gather(t, every):
        out = {}
        for o in (1, 2):
            cp = remote(every.at[0], every.at[o], gat_s.at[t, o], gat_r.at[t, o], mate_id[o])
            cp.start()
            out[o] = cp
        return out

    def relay(t, every, copies):
        out = []
        for o, lo_row in ((1, 0), (2, half)):
            copies[o].wait_recv()
            part = pl.ds(lo_row, half)
            cp = remote(every.at[o, part], every.at[3, part], rel_s.at[t, o], rel_r.at[t, o], mate_id[3 - o])
            cp.start()
            out.append(cp)
        return out

    def to_owner(t, parts, got):
        out = []
        for k in sibs:
            theirs = pl.ds(pl.multiple_of(sibs[k] * rows_own, rows_own), rows_own)
            cp = remote(parts.at[theirs], got.at[k - 1], red_s.at[t, k], red_r.at[t, k], sib_id[k])
            cp.start()
            out.append(cp)
        return out

    loads[0].wait()
    mask_into(x_raw, x_own)
    sib_x = share(0, x_own)
    loads[1].wait()
    mask_into(dy_raw, y_own)
    a2a_y = spread(1, y_own, y_all)
    sib_y = share(1, y_own)

    loads[2].wait()
    for cp in sib_x:
        cp.wait_recv()
    acc = None
    for l in range(GROUP):
        for h in range(steps):
            c = h * GROUP + l
            term = jnp.dot(x_own[l, h], wu[c * chunk:(c + 1) * chunk, :], preferred_element_type=F32)
            acc = term if acc is None else acc + term
    pre[...] = acc

    piece = 32

    def gelu_step(i, carry):
        r = pl.ds(pl.multiple_of(i * piece, piece), piece)
        value, sl = gelu_parts(pre[r, :])
        h_all[0, r, :] = (value * gate).astype(BF16)
        slope[r, :] = sl
        return carry

    lax.fori_loop(0, rows // piece, gelu_step, 0)
    gat_h = gather(0, h_all)
    a2a_x = spread(0, x_own, x_all)

    loads[3].wait()
    for cp in sib_y:
        cp.wait_recv()
    acc = None
    nt = (((1,), (1,)), ((), ()))
    for l in range(GROUP):
        for h in range(steps):
            c = h * GROUP + l
            term = lax.dot_general(
                y_own[l, h], wd[:, c * chunk:(c + 1) * chunk], nt, preferred_element_type=F32
            )
            acc = term if acc is None else acc + term
    g_all[0] = (acc * slope[...]).astype(BF16) * gate.astype(BF16)
    gat_g = gather(1, g_all)

    wide = 512

    def out_step(j, carry):
        cols = pl.ds(pl.multiple_of(j * wide, wide), wide)
        out_part[:, cols] = jnp.dot(h_all[0], wd[:, cols], preferred_element_type=F32).astype(BF16)
        return carry

    lax.fori_loop(0, feats // wide, out_step, 0)
    own_out = to_owner(0, out_part, out_got)
    h_t[:, 0:rows] = h_all[0].T
    for h in range(steps):
        y_all[h, 0] = y_own[lo, h]

    rel_h = relay(0, h_all, gat_h)
    fwd_y = forward(1, y_all, a2a_y)

    def in_step(j, carry):
        cols = pl.ds(pl.multiple_of(j * wide, wide), wide)
        in_part[:, cols] = lax.dot_general(
            g_all[0], wu[cols, :], nt, preferred_element_type=F32
        ).astype(BF16)
        return carry

    lax.fori_loop(0, feats // wide, in_step, 0)
    own_in = to_owner(1, in_part, in_got)
    g_t[:, 0:rows] = g_all[0].T
    for h in range(steps):
        x_all[h, 0] = x_own[lo, h]
    for o in (1, 2):
        h_t[:, o * rows:(o + 1) * rows] = h_all[o].T

    def finish(parts, got, raw, held, copies):
        for cp in copies:
            cp.wait_recv()

        def step(j, carry):
            cols = pl.ds(pl.multiple_of(j * wide, wide), wide)
            total = parts[mine, cols].astype(F32)
            for k in sibs:
                total = total + got[k - 1, :, cols].astype(F32)
            held[:, cols] = (raw[:, cols].astype(F32) + chunk_mask(j * wide, wide, F32) * total).astype(BF16)
            return carry

        lax.fori_loop(0, feats // wide, step, 0)

    finish(out_part, out_got, x_raw, mixed_v, own_out)
    store_mixed = pltpu.make_async_copy(mixed_v, mixed_hbm, loc.at[4])
    store_mixed.start()

    def partials(t, every_t, every):
        def step(h, carry):
            block = every[h].reshape(GROUP * rows, chunk)
            partial[t, h] = jnp.dot(every_t[...], block, preferred_element_type=F32)
            return carry

        lax.fori_loop(0, steps, step, 0)

    def z_copy(t, side, d):
        return remote(
            z_send.at[t, side, d - 1], z_got.at[t, side, d - 1], zs.at[t, side, d - 1], zr.at[t, side, d - 1],
            side_id[side],
        )

    def z_conditions(side, d):
        sends = hi + d <= steps - 1 if side == 0 else hi - d >= 0
        behind = has_left if side == 0 else has_right
        return sends, behind

    def chain(t):
        for d in range(steps - 1, 0, -1):
            for side in (0, 1):
                sends, behind = z_conditions(side, d)

                @pl.when(sends)
                def _():
                    target = hi + d if side == 0 else hi - d
                    if d == steps - 1:
                        z_send[t, side, d - 1] = partial[t, target].astype(BF16)
                    else:
                        @pl.when(behind)
                        def _():
                            z_copy(t, side, d + 1).wait_recv()
                            z_send[t, side, d - 1] = (
                                partial[t, target] + z_got[t, side, d].astype(F32)
                            ).astype(BF16)

                        @pl.when(jnp.logical_not(behind))
                        def _():
                            z_send[t, side, d - 1] = partial[t, target].astype(BF16)

                    z_copy(t, side, d).start()

    def close(t):
        for side, behind in ((0, has_left), (1, has_right)):
            @pl.when(behind)
            def _():
                z_copy(t, side, 1).wait_recv()
                partial[t, hi] = partial[t, hi] + z_got[t, side, 0].astype(F32)

        return partial[t, hi] * inv

    for cp in rel_h:
        cp.wait_recv()
    h_t[:, 3 * rows:] = h_all[3].T
    for cp in fwd_y:
        cp.wait_recv()
    partials(0, h_t, y_all)
    chain(0)

    rel_g = relay(1, g_all, gat_g)
    fwd_x = forward(0, x_all, a2a_x)
    for o in (1, 2):
        g_t[:, o * rows:(o + 1) * rows] = g_all[o].T
    finish(in_part, in_got, dy_raw, ing_v, own_in)
    store_ing = pltpu.make_async_copy(ing_v, ing_hbm, loc.at[5])
    store_ing.start()

    for cp in rel_g:
        cp.wait_recv()
    g_t[:, 3 * rows:] = g_all[3].T
    for cp in fwd_x:
        cp.wait_recv()
    partials(1, g_t, x_all)
    chain(1)

    grad_v[...] = close(0)
    store_down = pltpu.make_async_copy(grad_v, down_hbm, loc.at[6])
    store_down.start()
    pre_t = close(1)
    up_v = pre.at[0:chunk, :]
    up_v[...] = pre_t.T
    store_up = pltpu.make_async_copy(up_v, up_hbm, loc.at[7])
    store_up.start()

    for cp in sib_x + sib_y + own_out + own_in + fwd_x + fwd_y + rel_h + rel_g:
        cp.wait_send()
    for group in (a2a_x, a2a_y, gat_h, gat_g):
        for cp in group.values():
            cp.wait_send()
    for t in (0, 1):
        for d in range(steps - 1, 0, -1):
            for side in (0, 1):
                sends, _ = z_conditions(side, d)

                @pl.when(sends)
                def _():
                    z_copy(t, side, d).wait_send()
    for cp in (store_mixed, store_ing, store_down, store_up):
        cp.wait()


def local(n_dp, n_blk, tokens, cotangent, w_up, w_down, active, width, counts):
    _, rows_own, feats = tokens.shape
    units = w_up.shape[2]
    rows = rows_own * n_blk
    chunk = feats // n_dp
    steps = n_dp // GROUP
    hops = max(steps - 1, 1)
    dma = pltpu.SemaphoreType.DMA
    anywhere = pl.BlockSpec(memory_space=pl.ANY)
    scalars = pl.BlockSpec(memory_space=pltpu.SMEM)
    scratch = [
        pltpu.VMEM((rows_own, feats), BF16),
        pltpu.VMEM((rows_own, feats), BF16),
        pltpu.VMEM((feats, units), BF16),
        pltpu.VMEM((units, feats), BF16),
        pltpu.VMEM((GROUP, steps, rows, chunk), BF16),
        pltpu.VMEM((GROUP, steps, rows, chunk), BF16),
        pltpu.VMEM((steps, GROUP, rows, chunk), BF16),
        pltpu.VMEM((steps, GROUP, rows, chunk), BF16),
        pltpu.VMEM((GROUP, rows, units), BF16),
        pltpu.VMEM((GROUP, rows, units), BF16),
        pltpu.VMEM((units, GROUP * rows), BF16),
        pltpu.VMEM((units, GROUP * rows), BF16),
        pltpu.VMEM((rows, units), F32),
        pltpu.VMEM((rows, units), F32),
        pltpu.VMEM((rows, feats), BF16),
        pltpu.VMEM((rows, feats), BF16),
        pltpu.VMEM((n_blk - 1, rows_own, feats), BF16),
        pltpu.VMEM((n_blk - 1, rows_own, feats), BF16),
        pltpu.VMEM((2, steps, units, chunk), F32),
        pltpu.VMEM((2, 2, hops, units, chunk), BF16),
        pltpu.VMEM((2, 2, hops, units, chunk), BF16),
        pltpu.VMEM((rows_own, feats), BF16),
        pltpu.VMEM((rows_own, feats), BF16),
        pltpu.VMEM((units, chunk), F32),
        dma((8,)),
        dma((2, n_blk)), dma((2, n_blk)),
        dma((2, GROUP)), dma((2, GROUP)),
        dma((2, GROUP, n_blk)), dma((2, GROUP, n_blk)),
        dma((2, GROUP)), dma((2, GROUP)),
        dma((2, GROUP)), dma((2, GROUP)),
        dma((2, n_blk)), dma((2, n_blk)),
        dma((2, 2, hops)), dma((2, 2, hops)),
    ]
    mixed, ing, up, down = pl.pallas_call(
        functools.partial(kernel, n_dp, n_blk),
        out_shape=(
            jax.ShapeDtypeStruct((rows_own, feats), BF16),
            jax.ShapeDtypeStruct((rows_own, feats), BF16),
            jax.ShapeDtypeStruct((chunk, units), F32),
            jax.ShapeDtypeStruct((units, chunk), F32),
        ),
        in_specs=[anywhere] * 4 + [scalars] * 3,
        out_specs=(anywhere,) * 4,
        scratch_shapes=scratch,
        compiler_params=pltpu.CompilerParams(
            collective_id=0, has_side_effects=True, vmem_limit_bytes=60 * 1024 * 1024
        ),
        cost_estimate=pl.CostEstimate(
            flops=12 * rows * feats * units, bytes_accessed=16 * 1024 * 1024, transcendentals=rows * units
        ),
    )(tokens[0], cotangent[0], w_up[0], w_down[0], active, width, counts)
    return mixed[None], ing[None], up[None], down[None]


def solution(mesh):
    in_specs = (
        P("dp", "block", None),
        P("dp", "block", None),
        P("block", None, None),
        P("block", None, None),
        P(),
        P(),
        P(),
    )
    out_specs = (
        P("dp", "block", None),
        P("dp", "block", None),
        P("block", "dp", None),
        P("block", None, "dp"),
    )
    body = functools.partial(local, mesh.shape["dp"], mesh.shape["block"])
    return jax.shard_map(body, mesh=mesh, in_specs=in_specs, out_specs=out_specs, check_vma=False)
```

```python
import functools
import math

import jax
import jax.numpy as jnp
from jax import lax
from jax.experimental import pallas as pl
from jax.experimental.pallas import tpu as pltpu
from jax.sharding import PartitionSpec as P

GELU_C = math.sqrt(2.0 / math.pi)
GROUP = 4
BF16 = jnp.bfloat16
F32 = jnp.float32


def gelu_parts(v):
    t = jnp.tanh(GELU_C * (v + 0.044715 * v * v * v))
    value = 0.5 * v * (1.0 + t)
    slope = 0.5 * (1.0 + t) + 0.5 * v * (1.0 - t * t) * GELU_C * (1.0 + 3.0 * 0.044715 * v * v)
    return value, slope


def kernel(
    n_dp, n_blk,
    x_hbm, dy_hbm, wu_hbm, wd_hbm, active, width, counts,
    mixed_hbm, ing_hbm, up_hbm, down_hbm,
    x_raw, dy_raw, wu, wd, x_own, y_own, x_all, y_all, h_all, g_all, h_t, g_t, pre, slope,
    out_part, in_part, out_got, in_got, partial, z_send, z_got, mixed_v, ing_v, grad_v,
    loc, sib_s, sib_r, a2a_s, a2a_r, fwd_s, fwd_r, gat_s, gat_r, rel_s, rel_r, red_s, red_r, zs, zr,
):
    me = lax.axis_index("dp")
    blk = lax.axis_index("block")
    steps = n_dp // GROUP
    rows_own, feats = x_raw.shape
    units = wu.shape[1]
    rows = rows_own * n_blk
    half = rows // 2
    chunk = feats // n_dp
    hi = lax.div(me, GROUP)
    lo = lax.rem(me, GROUP)
    lx = lax.rem(lo, 2)
    ly = lax.div(lo, 2)

    def mate(o):
        px = 1 - lx if o & 1 else lx
        py = 1 - ly if o & 2 else ly
        return py * 2 + px

    def at(dp, b):
        return {"dp": dp, "block": b}

    mesh_id = pl.DeviceIdType.MESH
    mates = {o: mate(o) for o in range(1, GROUP)}
    mate_id = {o: at(hi * GROUP + mates[o], blk) for o in mates}
    sibs = {k: lax.rem(blk + k, n_blk) for k in range(1, n_blk)}
    sib_id = {k: at(me, sibs[k]) for k in sibs}
    side_id = (at(me + GROUP, blk), at(me - GROUP, blk))
    has_right = hi < steps - 1
    has_left = hi > 0
    mine = pl.ds(pl.multiple_of(blk * rows_own, rows_own), rows_own)

    loads = [
        pltpu.make_async_copy(s, d, loc.at[i])
        for i, (s, d) in enumerate(((x_hbm, x_raw), (dy_hbm, dy_raw), (wu_hbm, wu), (wd_hbm, wd)))
    ]
    loads[1].start()
    loads[0].start()

    barrier = pltpu.get_barrier_semaphore()
    for dev in list(mate_id.values()) + list(sib_id.values()):
        pl.semaphore_signal(barrier, inc=1, device_id=dev, device_id_type=mesh_id)

    @pl.when(has_right)
    def _():
        pl.semaphore_signal(barrier, inc=1, device_id=side_id[0], device_id_type=mesh_id)

    @pl.when(has_left)
    def _():
        pl.semaphore_signal(barrier, inc=1, device_id=side_id[1], device_id_type=mesh_id)

    def remote(src, dst, s, r, dev):
        return pltpu.make_async_remote_copy(
            src_ref=src, dst_ref=dst, send_sem=s, recv_sem=r, device_id=dev, device_id_type=mesh_id
        )

    limit = feats // 16 * width[me]
    gate = active[blk, me].astype(F32)
    inv = 1.0 / counts[blk].astype(F32)

    def chunk_mask(start, size, kind):
        col = lax.broadcasted_iota(jnp.int32, (1, size), 1) + start
        return jnp.where(col < limit, 1.0, 0.0).astype(kind)

    def mask_into(raw, own):
        for l in range(GROUP):
            for h in range(steps):
                c = h * GROUP + l
                own[l, h, mine, :] = raw[:, c * chunk:(c + 1) * chunk] * chunk_mask(c * chunk, chunk, BF16)

    def share(t, own):
        out = []
        for k in sibs:
            cp = remote(own.at[:, :, mine, :], own.at[:, :, mine, :], sib_s.at[t, k], sib_r.at[t, k], sib_id[k])
            cp.start()
            out.append(cp)
        return out

    def z_conditions(side, d):
        sends = hi + d <= steps - 1 if side == 0 else hi - d >= 0
        behind = has_left if side == 0 else has_right
        return sends, behind

    def in_order(visit):
        for d in range(steps - 1, 0, -1):
            for side in (0, 1):
                @pl.when(z_conditions(side, d)[0])
                def _():
                    visit(hi + d if side == 0 else hi - d)

        visit(hi)

    def a2a_copy(t, own, every, o, h):
        return remote(
            own.at[mates[o], h, mine, :], every.at[h, o, mine, :], a2a_s.at[t, o, h], a2a_r.at[t, o, h], mate_id[o]
        )

    def spread(t, own, every):
        def visit(h):
            for o in mates:
                a2a_copy(t, own, every, o, h).start()

        in_order(visit)

    def fwd_copy(t, every, o, h, k):
        part = every.at[h, o, mine, :]
        return remote(part, part, fwd_s.at[t, o, h, k], fwd_r.at[t, o, h, k], sib_id[k])

    def forward(t, own, every, h):
        for o in mates:
            a2a_copy(t, own, every, o, h).wait_recv()
            for k in sibs:
                fwd_copy(t, every, o, h, k).start()

    def forwarded(t, every, h):
        for o in mates:
            for k in sibs:
                fwd_copy(t, every, o, h, k).wait_recv()

    def gather(t, every):
        out = {}
        for o in (1, 2):
            cp = remote(every.at[0], every.at[o], gat_s.at[t, o], gat_r.at[t, o], mate_id[o])
            cp.start()
            out[o] = cp
        return out

    def relay(t, every, copies):
        out = []
        for o, lo_row in ((1, 0), (2, half)):
            copies[o].wait_recv()
            part = pl.ds(lo_row, half)
            cp = remote(every.at[o, part], every.at[3, part], rel_s.at[t, o], rel_r.at[t, o], mate_id[3 - o])
            cp.start()
            out.append(cp)
        return out

    def to_owner(t, parts, got):
        out = []
        for k in sibs:
            theirs = pl.ds(pl.multiple_of(sibs[k] * rows_own, rows_own), rows_own)
            cp = remote(parts.at[theirs], got.at[k - 1], red_s.at[t, k], red_r.at[t, k], sib_id[k])
            cp.start()
            out.append(cp)
        return out

    loads[1].wait()
    loads[2].start()
    loads[3].start()
    mask_into(dy_raw, y_own)
    pl.semaphore_wait(
        barrier,
        len(mate_id) + len(sib_id) + has_right.astype(jnp.int32) + has_left.astype(jnp.int32),
    )

    spread(1, y_own, y_all)
    loads[0].wait()
    mask_into(x_raw, x_own)
    sib_x = share(0, x_own)
    sib_y = share(1, y_own)

    loads[2].wait()
    for cp in sib_x:
        cp.wait_recv()
    acc = None
    for l in range(GROUP):
        for h in range(steps):
            c = h * GROUP + l
            term = jnp.dot(x_own[l, h], wu[c * chunk:(c + 1) * chunk, :], preferred_element_type=F32)
            acc = term if acc is None else acc + term
    pre[...] = acc

    piece = 32

    def gelu_step(i, carry):
        r = pl.ds(pl.multiple_of(i * piece, piece), piece)
        value, sl = gelu_parts(pre[r, :])
        h_all[0, r, :] = (value * gate).astype(BF16)
        slope[r, :] = sl
        return carry

    lax.fori_loop(0, rows // piece, gelu_step, 0)
    gat_h = gather(0, h_all)

    loads[3].wait()
    for cp in sib_y:
        cp.wait_recv()
    acc = None
    nt = (((1,), (1,)), ((), ()))
    for l in range(GROUP):
        for h in range(steps):
            c = h * GROUP + l
            term = lax.dot_general(
                y_own[l, h], wd[:, c * chunk:(c + 1) * chunk], nt, preferred_element_type=F32
            )
            acc = term if acc is None else acc + term
    g_all[0] = (acc * slope[...]).astype(BF16) * gate.astype(BF16)

    wide = 512

    def out_step(j, carry):
        cols = pl.ds(pl.multiple_of(j * wide, wide), wide)
        out_part[:, cols] = jnp.dot(h_all[0], wd[:, cols], preferred_element_type=F32).astype(BF16)
        return carry

    lax.fori_loop(0, feats // wide, out_step, 0)
    own_out = to_owner(0, out_part, out_got)
    h_t[:, 0:rows] = h_all[0].T
    for h in range(steps):
        y_all[h, 0] = y_own[lo, h]

    rel_h = relay(0, h_all, gat_h)
    gat_g = gather(1, g_all)

    def in_step(j, carry):
        cols = pl.ds(pl.multiple_of(j * wide, wide), wide)
        in_part[:, cols] = lax.dot_general(
            g_all[0], wu[cols, :], nt, preferred_element_type=F32
        ).astype(BF16)
        return carry

    lax.fori_loop(0, feats // wide, in_step, 0)
    own_in = to_owner(1, in_part, in_got)
    g_t[:, 0:rows] = g_all[0].T
    for h in range(steps):
        x_all[h, 0] = x_own[lo, h]
    for o in (1, 2):
        h_t[:, o * rows:(o + 1) * rows] = h_all[o].T

    def finish(parts, got, raw, held, copies):
        for cp in copies:
            cp.wait_recv()

        def step(j, carry):
            cols = pl.ds(pl.multiple_of(j * wide, wide), wide)
            total = parts[mine, cols].astype(F32)
            for k in sibs:
                total = total + got[k - 1, :, cols].astype(F32)
            held[:, cols] = (raw[:, cols].astype(F32) + chunk_mask(j * wide, wide, F32) * total).astype(BF16)
            return carry

        lax.fori_loop(0, feats // wide, step, 0)

    finish(out_part, out_got, x_raw, mixed_v, own_out)
    store_mixed = pltpu.make_async_copy(mixed_v, mixed_hbm, loc.at[4])
    store_mixed.start()

    def partial_of(t, h):
        if t == 0:
            each_t, own, every = h_t, y_own, y_all
        else:
            each_t, own, every = g_t, x_own, x_all
        forward(1 - t, own, every, h)
        forwarded(1 - t, every, h)
        return jnp.dot(each_t[...], every[h].reshape(GROUP * rows, chunk), preferred_element_type=F32)

    def z_copy(t, side, d):
        return remote(
            z_send.at[t, side, d - 1], z_got.at[t, side, d - 1], zs.at[t, side, d - 1], zr.at[t, side, d - 1],
            side_id[side],
        )

    def chain(t, between):
        for d in range(steps - 1, 0, -1):
            if d == 1:
                between()
            for side in (0, 1):
                sends, behind = z_conditions(side, d)

                @pl.when(sends)
                def _():
                    partial[t] = partial_of(t, hi + d if side == 0 else hi - d)
                    if d < steps - 1:
                        @pl.when(behind)
                        def _():
                            z_copy(t, side, d + 1).wait_recv()
                            partial[t] = partial[t] + z_got[t, side, d].astype(F32)

                    z_send[t, side, d - 1] = partial[t].astype(BF16)
                    z_copy(t, side, d).start()

        partial[t] = partial_of(t, hi)

    def close(t):
        for side, behind in ((0, has_left), (1, has_right)):
            @pl.when(behind)
            def _():
                z_copy(t, side, 1).wait_recv()
                partial[t] = partial[t] + z_got[t, side, 0].astype(F32)

        return partial[t] * inv

    def pass_on():
        rel_g.extend(relay(1, g_all, gat_g))
        spread(0, x_own, x_all)

    rel_g = []
    for cp in rel_h:
        cp.wait_recv()
    h_t[:, 3 * rows:] = h_all[3].T
    chain(0, pass_on)

    for o in (1, 2):
        g_t[:, o * rows:(o + 1) * rows] = g_all[o].T
    finish(in_part, in_got, dy_raw, ing_v, own_in)
    store_ing = pltpu.make_async_copy(ing_v, ing_hbm, loc.at[5])
    store_ing.start()

    for cp in rel_g:
        cp.wait_recv()
    g_t[:, 3 * rows:] = g_all[3].T
    chain(1, lambda: None)

    grad_v[...] = close(0)
    store_down = pltpu.make_async_copy(grad_v, down_hbm, loc.at[6])
    store_down.start()
    pre_t = close(1)
    up_v = pre.at[0:chunk, :]
    up_v[...] = pre_t.T
    store_up = pltpu.make_async_copy(up_v, up_hbm, loc.at[7])
    store_up.start()

    for cp in sib_x + sib_y + own_out + own_in + rel_h + rel_g:
        cp.wait_send()

    def drain(h, carry):
        for t, own, every in ((0, x_own, x_all), (1, y_own, y_all)):
            for o in mates:
                a2a_copy(t, own, every, o, h).wait_send()
                for k in sibs:
                    fwd_copy(t, every, o, h, k).wait_send()
        return carry

    lax.fori_loop(0, steps, drain, 0)
    for group in (gat_h, gat_g):
        for cp in group.values():
            cp.wait_send()
    for t in (0, 1):
        for d in range(steps - 1, 0, -1):
            for side in (0, 1):
                sends, _ = z_conditions(side, d)

                @pl.when(sends)
                def _():
                    z_copy(t, side, d).wait_send()
    for cp in (store_mixed, store_ing, store_down, store_up):
        cp.wait()


def hand_over(*refs):
    copies = []
    sems = refs[-1]
    for i in range(4):
        size = refs[i].shape[1] // 2
        for j in range(2):
            part = pl.ds(j * size, size)
            copies.append(pltpu.make_async_copy(refs[i].at[:, part], refs[4 + i].at[:, part], sems.at[i, j]))
    for cp in copies:
        cp.start()
    for cp in copies:
        cp.wait()


def local(n_dp, n_blk, tokens, cotangent, w_up, w_down, active, width, counts):
    _, rows_own, feats = tokens.shape
    units = w_up.shape[2]
    rows = rows_own * n_blk
    chunk = feats // n_dp
    steps = n_dp // GROUP
    hops = max(steps - 1, 1)
    dma = pltpu.SemaphoreType.DMA
    anywhere = pl.BlockSpec(memory_space=pl.ANY)
    scalars = pl.BlockSpec(memory_space=pltpu.SMEM)
    scratch = [
        pltpu.VMEM((rows_own, feats), BF16),
        pltpu.VMEM((rows_own, feats), BF16),
        pltpu.VMEM((feats, units), BF16),
        pltpu.VMEM((units, feats), BF16),
        pltpu.VMEM((GROUP, steps, rows, chunk), BF16),
        pltpu.VMEM((GROUP, steps, rows, chunk), BF16),
        pltpu.VMEM((steps, GROUP, rows, chunk), BF16),
        pltpu.VMEM((steps, GROUP, rows, chunk), BF16),
        pltpu.VMEM((GROUP, rows, units), BF16),
        pltpu.VMEM((GROUP, rows, units), BF16),
        pltpu.VMEM((units, GROUP * rows), BF16),
        pltpu.VMEM((units, GROUP * rows), BF16),
        pltpu.VMEM((rows, units), F32),
        pltpu.VMEM((rows, units), F32),
        pltpu.VMEM((rows, feats), BF16),
        pltpu.VMEM((rows, feats), BF16),
        pltpu.VMEM((n_blk - 1, rows_own, feats), BF16),
        pltpu.VMEM((n_blk - 1, rows_own, feats), BF16),
        pltpu.VMEM((2, units, chunk), F32),
        pltpu.VMEM((2, 2, hops, units, chunk), BF16),
        pltpu.VMEM((2, 2, hops, units, chunk), BF16),
        pltpu.VMEM((rows_own, feats), BF16),
        pltpu.VMEM((rows_own, feats), BF16),
        pltpu.VMEM((units, chunk), F32),
        dma((8,)),
        dma((2, n_blk)), dma((2, n_blk)),
        dma((2, GROUP, steps)), dma((2, GROUP, steps)),
        dma((2, GROUP, steps, n_blk)), dma((2, GROUP, steps, n_blk)),
        dma((2, GROUP)), dma((2, GROUP)),
        dma((2, GROUP)), dma((2, GROUP)),
        dma((2, n_blk)), dma((2, n_blk)),
        dma((2, 2, hops)), dma((2, 2, hops)),
    ]
    mixed, ing, up, down = pl.pallas_call(
        functools.partial(kernel, n_dp, n_blk),
        out_shape=(
            jax.ShapeDtypeStruct((rows_own, feats), BF16),
            jax.ShapeDtypeStruct((rows_own, feats), BF16),
            jax.ShapeDtypeStruct((chunk, units), F32),
            jax.ShapeDtypeStruct((units, chunk), F32),
        ),
        in_specs=[anywhere] * 4 + [scalars] * 3,
        out_specs=(anywhere,) * 4,
        scratch_shapes=scratch,
        compiler_params=pltpu.CompilerParams(
            collective_id=0, has_side_effects=True, vmem_limit_bytes=60 * 1024 * 1024
        ),
        cost_estimate=pl.CostEstimate(
            flops=12 * rows * feats * units, bytes_accessed=16 * 1024 * 1024, transcendentals=rows * units
        ),
    )(tokens[0], cotangent[0], w_up[0], w_down[0], active.T, width, counts)
    results = (mixed[None], ing[None], up[None], down[None])
    return pl.pallas_call(
        hand_over,
        out_shape=tuple(jax.ShapeDtypeStruct(r.shape, r.dtype) for r in results),
        in_specs=[anywhere] * 4,
        out_specs=(anywhere,) * 4,
        scratch_shapes=[dma((4, 2))],
    )(*results)


def solution(mesh):
    in_specs = (
        P("dp", "block", None),
        P("dp", "block", None),
        P("block", None, None),
        P("block", None, None),
        P(),
        P(),
        P(),
    )
    out_specs = (
        P("dp", "block", None),
        P("dp", "block", None),
        P("block", "dp", None),
        P("block", None, "dp"),
    )
    body = functools.partial(local, mesh.shape["dp"], mesh.shape["block"])
    return jax.shard_map(body, mesh=mesh, in_specs=in_specs, out_specs=out_specs, check_vma=False)
```

```python
import functools
import math

import jax
import jax.numpy as jnp
from jax import lax
from jax.experimental import pallas as pl
from jax.experimental.pallas import tpu as pltpu
from jax.sharding import PartitionSpec as P

GELU_C = math.sqrt(2.0 / math.pi)
GROUP = 4
BF16 = jnp.bfloat16
F32 = jnp.float32


def gelu_parts(v):
    t = jnp.tanh(GELU_C * (v + 0.044715 * v * v * v))
    value = 0.5 * v * (1.0 + t)
    slope = 0.5 * (1.0 + t) + 0.5 * v * (1.0 - t * t) * GELU_C * (1.0 + 3.0 * 0.044715 * v * v)
    return value, slope


def kernel(
    n_dp, n_blk,
    x_hbm, dy_hbm, wu_hbm, wd_hbm, active, width, counts,
    mixed_hbm, ing_hbm, up_hbm, down_hbm,
    x_raw, dy_raw, wu, wd, x_own, y_own, x_all, y_all, h_all, g_all, h_t, g_t, pre, slope,
    out_part, in_part, out_got, in_got, partial, z_send, z_got, mixed_v, ing_v, grad_v,
    loc, sib_s, sib_r, a2a_s, a2a_r, fwd_s, fwd_r, gat_s, gat_r, rel_s, rel_r, red_s, red_r, zs, zr,
):
    me = lax.axis_index("dp")
    blk = lax.axis_index("block")
    steps = n_dp // GROUP
    rows_own, feats = x_raw.shape
    units = wu.shape[1]
    rows = rows_own * n_blk
    half = rows // 2
    wing = units // 2
    chunk = feats // n_dp
    hi = lax.div(me, GROUP)
    lo = lax.rem(me, GROUP)
    lx = lax.rem(lo, 2)
    ly = lax.div(lo, 2)

    def mate(o):
        px = 1 - lx if o & 1 else lx
        py = 1 - ly if o & 2 else ly
        return py * 2 + px

    def at(dp, b):
        return {"dp": dp, "block": b}

    mesh_id = pl.DeviceIdType.MESH
    mates = {o: mate(o) for o in range(1, GROUP)}
    mate_id = {o: at(hi * GROUP + mates[o], blk) for o in mates}
    sibs = {k: lax.rem(blk + k, n_blk) for k in range(1, n_blk)}
    sib_id = {k: at(me, sibs[k]) for k in sibs}
    side_id = (at(me + GROUP, blk), at(me - GROUP, blk))
    has_right = hi < steps - 1
    has_left = hi > 0
    mine = pl.ds(pl.multiple_of(blk * rows_own, rows_own), rows_own)

    loads = [
        pltpu.make_async_copy(s, d, loc.at[i])
        for i, (s, d) in enumerate(((x_hbm, x_raw), (dy_hbm, dy_raw), (wu_hbm, wu), (wd_hbm, wd)))
    ]
    loads[0].start()
    loads[1].start()

    barrier = pltpu.get_barrier_semaphore()
    for dev in list(mate_id.values()) + list(sib_id.values()):
        pl.semaphore_signal(barrier, inc=1, device_id=dev, device_id_type=mesh_id)

    @pl.when(has_right)
    def _():
        pl.semaphore_signal(barrier, inc=1, device_id=side_id[0], device_id_type=mesh_id)

    @pl.when(has_left)
    def _():
        pl.semaphore_signal(barrier, inc=1, device_id=side_id[1], device_id_type=mesh_id)

    def remote(src, dst, s, r, dev):
        return pltpu.make_async_remote_copy(
            src_ref=src, dst_ref=dst, send_sem=s, recv_sem=r, device_id=dev, device_id_type=mesh_id
        )

    limit = feats // 16 * width[me]
    gate = active[blk, me].astype(F32)
    inv = 1.0 / counts[blk].astype(F32)

    def chunk_mask(start, size, kind):
        col = lax.broadcasted_iota(jnp.int32, (1, size), 1) + start
        return jnp.where(col < limit, 1.0, 0.0).astype(kind)

    def mask_into(raw, own):
        for l in range(GROUP):
            for h in range(steps):
                c = h * GROUP + l
                own[l, h, mine, :] = raw[:, c * chunk:(c + 1) * chunk] * chunk_mask(c * chunk, chunk, BF16)

    def share(t, own):
        out = []
        for k in sibs:
            cp = remote(own.at[:, :, mine, :], own.at[:, :, mine, :], sib_s.at[t, k], sib_r.at[t, k], sib_id[k])
            cp.start()
            out.append(cp)
        return out

    def z_conditions(side, d):
        sends = hi + d <= steps - 1 if side == 0 else hi - d >= 0
        behind = has_left if side == 0 else has_right
        return sends, behind

    near = steps // 2
    low = (hi < near).astype(jnp.int32)
    base = (1 - low) * near
    order = [low * (steps - 1 - i) + (1 - low) * i for i in range(near)]
    order += [base + lax.rem(hi - base + 1 + i, near) for i in range(near)]

    def a2a_copy(t, own, every, o, h):
        return remote(
            own.at[mates[o], h, mine, :], every.at[h, o, mine, :], a2a_s.at[t, o, h], a2a_r.at[t, o, h], mate_id[o]
        )

    def spread(t, own, every, targets):
        for h in targets:
            for o in mates:
                a2a_copy(t, own, every, o, h).start()

    def fwd_copy(t, every, o, h, k):
        part = every.at[h, o, mine, :]
        return remote(part, part, fwd_s.at[t, o, h, k], fwd_r.at[t, o, h, k], sib_id[k])

    def forward(t, own, every, h):
        for o in mates:
            a2a_copy(t, own, every, o, h).wait_recv()
            for k in sibs:
                fwd_copy(t, every, o, h, k).start()

    def forwarded(t, every, h):
        for o in mates:
            for k in sibs:
                fwd_copy(t, every, o, h, k).wait_recv()

    def gather(t, every):
        out = {}
        for u in (0, 1):
            for o in (1, 2):
                cp = remote(every.at[u, 0], every.at[u, o], gat_s.at[t, u, o], gat_r.at[t, u, o], mate_id[o])
                cp.start()
                out[u, o] = cp
        return out

    def relay(t, u, every, copies):
        out = []
        for o, lo_row in ((1, 0), (2, half)):
            copies[u, o].wait_recv()
            part = pl.ds(lo_row, half)
            cp = remote(
                every.at[u, o, part], every.at[u, 3, part], rel_s.at[t, u, o], rel_r.at[t, u, o], mate_id[3 - o]
            )
            cp.start()
            out.append(cp)
        return out

    def turn(u, every, every_t, slots):
        for o in slots:
            every_t[u, :, o * rows:(o + 1) * rows] = every[u, o].T

    def to_owner(t, parts, got):
        out = []
        for k in sibs:
            theirs = pl.ds(pl.multiple_of(sibs[k] * rows_own, rows_own), rows_own)
            cp = remote(parts.at[theirs], got.at[k - 1], red_s.at[t, k], red_r.at[t, k], sib_id[k])
            cp.start()
            out.append(cp)
        return out

    loads[0].wait()
    loads[2].start()
    mask_into(x_raw, x_own)
    pl.semaphore_wait(
        barrier,
        len(mate_id) + len(sib_id) + has_right.astype(jnp.int32) + has_left.astype(jnp.int32),
    )

    sib_x = share(0, x_own)
    loads[1].wait()
    loads[3].start()
    mask_into(dy_raw, y_own)
    spread(1, y_own, y_all, order[:-1])
    sib_y = share(1, y_own)

    loads[2].wait()
    for cp in sib_x:
        cp.wait_recv()
    acc = None
    for l in range(GROUP):
        for h in range(steps):
            c = h * GROUP + l
            term = jnp.dot(x_own[l, h], wu[c * chunk:(c + 1) * chunk, :], preferred_element_type=F32)
            acc = term if acc is None else acc + term
    pre[...] = acc

    piece = 32

    def gelu_step(i, carry):
        r = pl.ds(pl.multiple_of(i * piece, piece), piece)
        value, sl = gelu_parts(pre[r, :])
        value = (value * gate).astype(BF16)
        h_all[0, 0, r, :] = value[:, :wing]
        h_all[1, 0, r, :] = value[:, wing:]
        slope[r, :] = sl
        return carry

    lax.fori_loop(0, rows // piece, gelu_step, 0)
    gat_h = gather(0, h_all)

    loads[3].wait()
    for cp in sib_y:
        cp.wait_recv()
    acc = None
    nt = (((1,), (1,)), ((), ()))
    for l in range(GROUP):
        for h in range(steps):
            c = h * GROUP + l
            term = lax.dot_general(
                y_own[l, h], wd[:, c * chunk:(c + 1) * chunk], nt, preferred_element_type=F32
            )
            acc = term if acc is None else acc + term
    grad = (acc * slope[...]).astype(BF16) * gate.astype(BF16)
    g_all[0, 0] = grad[:, :wing]
    g_all[1, 0] = grad[:, wing:]
    for u in (0, 1):
        turn(u, h_all, h_t, (0,))
    for h in range(steps):
        y_all[h, 0] = y_own[lo, h]

    rel_h = [relay(0, u, h_all, gat_h) for u in (0, 1)]
    spread(1, y_own, y_all, order[-1:])
    gat_g = gather(1, g_all)
    turn(0, h_all, h_t, (1, 2))

    wide = 512

    def out_step(j, carry):
        cols = pl.ds(pl.multiple_of(j * wide, wide), wide)
        total = jnp.dot(h_all[0, 0], wd[0:wing, cols], preferred_element_type=F32)
        total = total + jnp.dot(h_all[1, 0], wd[wing:, cols], preferred_element_type=F32)
        out_part[:, cols] = total.astype(BF16)
        return carry

    def in_step(j, carry):
        cols = pl.ds(pl.multiple_of(j * wide, wide), wide)
        total = lax.dot_general(g_all[0, 0], wu[cols, 0:wing], nt, preferred_element_type=F32)
        total = total + lax.dot_general(g_all[1, 0], wu[cols, wing:], nt, preferred_element_type=F32)
        in_part[:, cols] = total.astype(BF16)
        return carry

    def finish(parts, got, raw, held, copies):
        for cp in copies:
            cp.wait_recv()

        def step(j, carry):
            cols = pl.ds(pl.multiple_of(j * wide, wide), wide)
            total = parts[mine, cols].astype(F32)
            for k in sibs:
                total = total + got[k - 1, :, cols].astype(F32)
            held[:, cols] = (raw[:, cols].astype(F32) + chunk_mask(j * wide, wide, F32) * total).astype(BF16)
            return carry

        lax.fori_loop(0, feats // wide, step, 0)

    def partial_of(t, u, h):
        if t == 0:
            each_t, own, every = h_t, y_own, y_all
        else:
            each_t, own, every = g_t, x_own, x_all
        if u == 0:
            forward(1 - t, own, every, h)
            forwarded(1 - t, every, h)
        return jnp.dot(each_t[u], every[h].reshape(GROUP * rows, chunk), preferred_element_type=F32)

    def z_copy(q, side, d):
        return remote(
            z_send.at[q, side, d - 1], z_got.at[q, side, d - 1], zs.at[q, side, d - 1], zr.at[q, side, d - 1],
            side_id[side],
        )

    def chain(t, u, between):
        q = 2 * t + u
        for d in range(steps - 1, 0, -1):
            if d == 1:
                between()
            for side in (0, 1):
                sends, behind = z_conditions(side, d)

                @pl.when(sends)
                def _():
                    partial[q] = partial_of(t, u, hi + d if side == 0 else hi - d)
                    if d < steps - 1:
                        @pl.when(behind)
                        def _():
                            z_copy(q, side, d + 1).wait_recv()
                            partial[q] = partial[q] + z_got[q, side, d].astype(F32)

                    z_send[q, side, d - 1] = partial[q].astype(BF16)
                    z_copy(q, side, d).start()

        partial[q] = partial_of(t, u, hi)

    def close(q):
        for side, behind in ((0, has_left), (1, has_right)):
            @pl.when(behind)
            def _():
                z_copy(q, side, 1).wait_recv()
                partial[q] = partial[q] + z_got[q, side, 0].astype(F32)

        return partial[q] * inv

    def arrived(t, u, every, every_t, copies):
        for cp in copies:
            cp.wait_recv()
        turn(u, every, every_t, (3,))

    rel_g = []

    def pass_on():
        for u in (0, 1):
            rel_g.append(relay(1, u, g_all, gat_g))
        spread(0, x_own, x_all, order)

    def nothing():
        pass

    arrived(0, 0, h_all, h_t, rel_h[0])
    chain(0, 0, nothing)
    lax.fori_loop(0, feats // wide, out_step, 0)
    own_out = to_owner(0, out_part, out_got)
    turn(1, h_all, h_t, (1, 2))
    for u in (0, 1):
        turn(u, g_all, g_t, (0,))
    for h in range(steps):
        x_all[h, 0] = x_own[lo, h]
    arrived(0, 1, h_all, h_t, rel_h[1])
    chain(0, 1, pass_on)
    lax.fori_loop(0, feats // wide, in_step, 0)
    own_in = to_owner(1, in_part, in_got)
    turn(0, g_all, g_t, (1, 2))
    arrived(1, 0, g_all, g_t, rel_g[0])
    chain(1, 0, nothing)
    turn(1, g_all, g_t, (1, 2))
    arrived(1, 1, g_all, g_t, rel_g[1])
    finish(out_part, out_got, x_raw, mixed_v, own_out)
    store_mixed = pltpu.make_async_copy(mixed_v, mixed_hbm, loc.at[4])
    store_mixed.start()
    chain(1, 1, nothing)
    finish(in_part, in_got, dy_raw, ing_v, own_in)
    store_ing = pltpu.make_async_copy(ing_v, ing_hbm, loc.at[5])
    store_ing.start()

    grad_v[0:wing] = close(0)
    grad_v[wing:] = close(1)
    store_down = pltpu.make_async_copy(grad_v, down_hbm, loc.at[6])
    store_down.start()
    up_v = pre.at[0:chunk, :]
    pre[0:chunk, 0:wing] = close(2).T
    pre[0:chunk, wing:] = close(3).T
    store_up = pltpu.make_async_copy(up_v, up_hbm, loc.at[7])
    store_up.start()

    for cp in sib_x + sib_y + own_out + own_in + sum(rel_h + rel_g, []):
        cp.wait_send()

    def drain(h, carry):
        for t, own, every in ((0, x_own, x_all), (1, y_own, y_all)):
            for o in mates:
                a2a_copy(t, own, every, o, h).wait_send()
                for k in sibs:
                    fwd_copy(t, every, o, h, k).wait_send()
        return carry

    lax.fori_loop(0, steps, drain, 0)
    for group in (gat_h, gat_g):
        for cp in group.values():
            cp.wait_send()
    for q in range(4):
        for d in range(steps - 1, 0, -1):
            for side in (0, 1):
                sends, _ = z_conditions(side, d)

                @pl.when(sends)
                def _():
                    z_copy(q, side, d).wait_send()
    for cp in (store_mixed, store_ing, store_down, store_up):
        cp.wait()


def hand_over(*refs):
    held, sems = refs[8:12], refs[12]
    parts = []
    for i in range(4):
        size = refs[i].shape[1] // 2
        parts += [(i, j, pl.ds(j * size, size)) for j in range(2)]
    reads = [pltpu.make_async_copy(refs[i].at[:, p], held[i].at[:, p], sems.at[0, i, j]) for i, j, p in parts]
    writes = [pltpu.make_async_copy(held[i].at[:, p], refs[4 + i].at[:, p], sems.at[1, i, j]) for i, j, p in parts]
    for cp in reads:
        cp.start()
    for get, put in zip(reads, writes):
        get.wait()
        put.start()
    for cp in writes:
        cp.wait()


def local(n_dp, n_blk, tokens, cotangent, w_up, w_down, active, width, counts):
    _, rows_own, feats = tokens.shape
    units = w_up.shape[2]
    rows = rows_own * n_blk
    chunk = feats // n_dp
    steps = n_dp // GROUP
    hops = max(steps - 1, 1)
    dma = pltpu.SemaphoreType.DMA
    anywhere = pl.BlockSpec(memory_space=pl.ANY)
    scalars = pl.BlockSpec(memory_space=pltpu.SMEM)
    scratch = [
        pltpu.VMEM((rows_own, feats), BF16),
        pltpu.VMEM((rows_own, feats), BF16),
        pltpu.VMEM((feats, units), BF16),
        pltpu.VMEM((units, feats), BF16),
        pltpu.VMEM((GROUP, steps, rows, chunk), BF16),
        pltpu.VMEM((GROUP, steps, rows, chunk), BF16),
        pltpu.VMEM((steps, GROUP, rows, chunk), BF16),
        pltpu.VMEM((steps, GROUP, rows, chunk), BF16),
        pltpu.VMEM((2, GROUP, rows, units // 2), BF16),
        pltpu.VMEM((2, GROUP, rows, units // 2), BF16),
        pltpu.VMEM((2, units // 2, GROUP * rows), BF16),
        pltpu.VMEM((2, units // 2, GROUP * rows), BF16),
        pltpu.VMEM((rows, units), F32),
        pltpu.VMEM((rows, units), F32),
        pltpu.VMEM((rows, feats), BF16),
        pltpu.VMEM((rows, feats), BF16),
        pltpu.VMEM((n_blk - 1, rows_own, feats), BF16),
        pltpu.VMEM((n_blk - 1, rows_own, feats), BF16),
        pltpu.VMEM((4, units // 2, chunk), F32),
        pltpu.VMEM((4, 2, hops, units // 2, chunk), BF16),
        pltpu.VMEM((4, 2, hops, units // 2, chunk), BF16),
        pltpu.VMEM((rows_own, feats), BF16),
        pltpu.VMEM((rows_own, feats), BF16),
        pltpu.VMEM((units, chunk), F32),
        dma((8,)),
        dma((2, n_blk)), dma((2, n_blk)),
        dma((2, GROUP, steps)), dma((2, GROUP, steps)),
        dma((2, GROUP, steps, n_blk)), dma((2, GROUP, steps, n_blk)),
        dma((2, 2, GROUP)), dma((2, 2, GROUP)),
        dma((2, 2, GROUP)), dma((2, 2, GROUP)),
        dma((2, n_blk)), dma((2, n_blk)),
        dma((4, 2, hops)), dma((4, 2, hops)),
    ]
    mixed, ing, up, down = pl.pallas_call(
        functools.partial(kernel, n_dp, n_blk),
        out_shape=(
            jax.ShapeDtypeStruct((rows_own, feats), BF16),
            jax.ShapeDtypeStruct((rows_own, feats), BF16),
            jax.ShapeDtypeStruct((chunk, units), F32),
            jax.ShapeDtypeStruct((units, chunk), F32),
        ),
        in_specs=[anywhere] * 4 + [scalars] * 3,
        out_specs=(anywhere,) * 4,
        scratch_shapes=scratch,
        compiler_params=pltpu.CompilerParams(
            collective_id=0, has_side_effects=True, vmem_limit_bytes=60 * 1024 * 1024
        ),
        cost_estimate=pl.CostEstimate(
            flops=12 * rows * feats * units, bytes_accessed=16 * 1024 * 1024, transcendentals=rows * units
        ),
    )(tokens[0], cotangent[0], w_up[0], w_down[0], active.T, width, counts)
    results = (mixed[None], ing[None], up[None], down[None])
    return pl.pallas_call(
        hand_over,
        out_shape=tuple(jax.ShapeDtypeStruct(r.shape, r.dtype) for r in results),
        in_specs=[anywhere] * 4,
        out_specs=(anywhere,) * 4,
        scratch_shapes=[pltpu.VMEM(r.shape, r.dtype) for r in results] + [dma((2, 4, 2))],
        compiler_params=pltpu.CompilerParams(vmem_limit_bytes=16 * 1024 * 1024),
    )(*results)


def solution(mesh):
    in_specs = (
        P("dp", "block", None),
        P("dp", "block", None),
        P("block", None, None),
        P("block", None, None),
        P(),
        P(),
        P(),
    )
    out_specs = (
        P("dp", "block", None),
        P("dp", "block", None),
        P("block", "dp", None),
        P("block", None, "dp"),
    )
    body = functools.partial(local, mesh.shape["dp"], mesh.shape["block"])
    return jax.shard_map(body, mesh=mesh, in_specs=in_specs, out_specs=out_specs, check_vma=False)
```

```python
import functools
import math

import jax
import jax.numpy as jnp
from jax import lax
from jax.experimental import pallas as pl
from jax.experimental.pallas import tpu as pltpu
from jax.sharding import PartitionSpec as P

GELU_C = math.sqrt(2.0 / math.pi)
GROUP = 4
BF16 = jnp.bfloat16
F32 = jnp.float32


def gelu_parts(v):
    t = jnp.tanh(GELU_C * (v + 0.044715 * v * v * v))
    value = 0.5 * v * (1.0 + t)
    slope = 0.5 * (1.0 + t) + 0.5 * v * (1.0 - t * t) * GELU_C * (1.0 + 3.0 * 0.044715 * v * v)
    return value, slope


def kernel(
    n_dp, n_blk,
    x_hbm, dy_hbm, wu_hbm, wd_hbm, active, width, counts,
    mixed_hbm, ing_hbm, up_hbm, down_hbm,
    x_raw, dy_raw, wu, wd, x_own, y_own, x_all, y_all, h_all, g_all, h_t, g_t, pre, slope,
    out_part, in_part, out_got, in_got, partial, z_send, z_got, mixed_v, ing_v, grad_v,
    loc, sib_s, sib_r, a2a_s, a2a_r, fwd_s, fwd_r, gat_s, gat_r, rel_s, rel_r, red_s, red_r, zs, zr,
):
    me = lax.axis_index("dp")
    blk = lax.axis_index("block")
    steps = n_dp // GROUP
    rows_own, feats = x_raw.shape
    units = wu.shape[1]
    rows = rows_own * n_blk
    half = rows // 2
    wing = units // 2
    chunk = feats // n_dp
    hi = lax.div(me, GROUP)
    lo = lax.rem(me, GROUP)
    lx = lax.rem(lo, 2)
    ly = lax.div(lo, 2)

    def mate(o):
        px = 1 - lx if o & 1 else lx
        py = 1 - ly if o & 2 else ly
        return py * 2 + px

    def at(dp, b):
        return {"dp": dp, "block": b}

    mesh_id = pl.DeviceIdType.MESH
    mates = {o: mate(o) for o in range(1, GROUP)}
    mate_id = {o: at(hi * GROUP + mates[o], blk) for o in mates}
    sibs = {k: lax.rem(blk + k, n_blk) for k in range(1, n_blk)}
    sib_id = {k: at(me, sibs[k]) for k in sibs}
    side_id = (at(me + GROUP, blk), at(me - GROUP, blk))
    has_right = hi < steps - 1
    has_left = hi > 0
    mine = pl.ds(pl.multiple_of(blk * rows_own, rows_own), rows_own)

    loads = [
        pltpu.make_async_copy(s, d, loc.at[i])
        for i, (s, d) in enumerate(((x_hbm, x_raw), (dy_hbm, dy_raw), (wu_hbm, wu), (wd_hbm, wd)))
    ]
    loads[0].start()
    loads[1].start()

    barrier = pltpu.get_barrier_semaphore()
    for dev in list(mate_id.values()) + list(sib_id.values()):
        pl.semaphore_signal(barrier, inc=1, device_id=dev, device_id_type=mesh_id)

    @pl.when(has_right)
    def _():
        pl.semaphore_signal(barrier, inc=1, device_id=side_id[0], device_id_type=mesh_id)

    @pl.when(has_left)
    def _():
        pl.semaphore_signal(barrier, inc=1, device_id=side_id[1], device_id_type=mesh_id)

    def remote(src, dst, s, r, dev):
        return pltpu.make_async_remote_copy(
            src_ref=src, dst_ref=dst, send_sem=s, recv_sem=r, device_id=dev, device_id_type=mesh_id
        )

    limit = feats // 16 * width[me]
    gate = active[blk, me].astype(F32)
    inv = 1.0 / counts[blk].astype(F32)

    def chunk_mask(start, size, kind):
        col = lax.broadcasted_iota(jnp.int32, (1, size), 1) + start
        return jnp.where(col < limit, 1.0, 0.0).astype(kind)

    def mask_into(raw, own):
        for l in range(GROUP):
            for h in range(steps):
                c = h * GROUP + l
                own[l, h, mine, :] = raw[:, c * chunk:(c + 1) * chunk] * chunk_mask(c * chunk, chunk, BF16)

    def share(t, own):
        out = []
        for k in sibs:
            cp = remote(own.at[:, :, mine, :], own.at[:, :, mine, :], sib_s.at[t, k], sib_r.at[t, k], sib_id[k])
            cp.start()
            out.append(cp)
        return out

    def z_conditions(side, d):
        sends = hi + d <= steps - 1 if side == 0 else hi - d >= 0
        behind = has_left if side == 0 else has_right
        return sends, behind

    near = steps // 2
    low = (hi < near).astype(jnp.int32)
    base = (1 - low) * near
    order = [low * (steps - 1 - i) + (1 - low) * i for i in range(near)]
    order += [base + lax.rem(hi - base + 1 + i, near) for i in range(near)]

    def a2a_copy(t, own, every, o, h):
        return remote(
            own.at[mates[o], h, mine, :], every.at[h, o, mine, :], a2a_s.at[t, o, h], a2a_r.at[t, o, h], mate_id[o]
        )

    def spread(t, own, every, targets):
        for h in targets:
            for o in mates:
                a2a_copy(t, own, every, o, h).start()

    def fwd_copy(t, every, o, h, k):
        part = every.at[h, o, mine, :]
        return remote(part, part, fwd_s.at[t, o, h, k], fwd_r.at[t, o, h, k], sib_id[k])

    def forward(t, own, every, h):
        for o in mates:
            a2a_copy(t, own, every, o, h).wait_recv()
            for k in sibs:
                fwd_copy(t, every, o, h, k).start()

    def forwarded(t, every, h):
        for o in mates:
            for k in sibs:
                fwd_copy(t, every, o, h, k).wait_recv()

    def gather(t, every):
        out = {}
        for u in (0, 1):
            for o in (1, 2):
                cp = remote(every.at[u, 0], every.at[u, o], gat_s.at[t, u, o], gat_r.at[t, u, o], mate_id[o])
                cp.start()
                out[u, o] = cp
        return out

    def relay(t, u, every, copies):
        out = []
        for o, lo_row in ((1, 0), (2, half)):
            copies[u, o].wait_recv()
            part = pl.ds(lo_row, half)
            cp = remote(
                every.at[u, o, part], every.at[u, 3, part], rel_s.at[t, u, o], rel_r.at[t, u, o], mate_id[3 - o]
            )
            cp.start()
            out.append(cp)
        return out

    def turn(u, every, every_t, slots):
        for o in slots:
            every_t[u, :, o * rows:(o + 1) * rows] = every[u, o].T

    def to_owner(t, parts, got):
        out = []
        for k in sibs:
            theirs = pl.ds(pl.multiple_of(sibs[k] * rows_own, rows_own), rows_own)
            cp = remote(parts.at[theirs], got.at[k - 1], red_s.at[t, k], red_r.at[t, k], sib_id[k])
            cp.start()
            out.append(cp)
        return out

    loads[0].wait()
    loads[2].start()
    mask_into(x_raw, x_own)
    pl.semaphore_wait(
        barrier,
        len(mate_id) + len(sib_id) + has_right.astype(jnp.int32) + has_left.astype(jnp.int32),
    )

    sib_x = share(0, x_own)
    loads[1].wait()
    loads[3].start()
    mask_into(dy_raw, y_own)
    spread(1, y_own, y_all, order[:-1])
    sib_y = share(1, y_own)

    loads[2].wait()
    for cp in sib_x:
        cp.wait_recv()
    acc = None
    for l in range(GROUP):
        for h in range(steps):
            c = h * GROUP + l
            term = jnp.dot(x_own[l, h], wu[c * chunk:(c + 1) * chunk, :], preferred_element_type=F32)
            acc = term if acc is None else acc + term
    pre[...] = acc

    piece = 32

    def gelu_step(i, carry):
        r = pl.ds(pl.multiple_of(i * piece, piece), piece)
        value, sl = gelu_parts(pre[r, :])
        value = (value * gate).astype(BF16)
        h_all[0, 0, r, :] = value[:, :wing]
        h_all[1, 0, r, :] = value[:, wing:]
        slope[r, :] = sl
        return carry

    lax.fori_loop(0, rows // piece, gelu_step, 0)
    gat_h = gather(0, h_all)

    loads[3].wait()
    for cp in sib_y:
        cp.wait_recv()
    acc = None
    nt = (((1,), (1,)), ((), ()))
    for l in range(GROUP):
        for h in range(steps):
            c = h * GROUP + l
            term = lax.dot_general(
                y_own[l, h], wd[:, c * chunk:(c + 1) * chunk], nt, preferred_element_type=F32
            )
            acc = term if acc is None else acc + term
    grad = (acc * slope[...]).astype(BF16) * gate.astype(BF16)
    g_all[0, 0] = grad[:, :wing]
    g_all[1, 0] = grad[:, wing:]
    for u in (0, 1):
        turn(u, h_all, h_t, (0,))
    for h in range(steps):
        y_all[h, 0] = y_own[lo, h]

    rel_h = [relay(0, u, h_all, gat_h) for u in (0, 1)]
    spread(1, y_own, y_all, order[-1:])
    gat_g = gather(1, g_all)
    turn(0, h_all, h_t, (1, 2))

    wide = 512

    def out_step(j, carry):
        cols = pl.ds(pl.multiple_of(j * wide, wide), wide)
        total = jnp.dot(h_all[0, 0], wd[0:wing, cols], preferred_element_type=F32)
        total = total + jnp.dot(h_all[1, 0], wd[wing:, cols], preferred_element_type=F32)
        out_part[:, cols] = total.astype(BF16)
        return carry

    def in_step(j, carry):
        cols = pl.ds(pl.multiple_of(j * wide, wide), wide)
        total = lax.dot_general(g_all[0, 0], wu[cols, 0:wing], nt, preferred_element_type=F32)
        total = total + lax.dot_general(g_all[1, 0], wu[cols, wing:], nt, preferred_element_type=F32)
        in_part[:, cols] = total.astype(BF16)
        return carry

    def finish(parts, got, raw, held, copies):
        for cp in copies:
            cp.wait_recv()

        def step(j, carry):
            cols = pl.ds(pl.multiple_of(j * wide, wide), wide)
            total = parts[mine, cols].astype(F32)
            for k in sibs:
                total = total + got[k - 1, :, cols].astype(F32)
            held[:, cols] = (raw[:, cols].astype(F32) + chunk_mask(j * wide, wide, F32) * total).astype(BF16)
            return carry

        lax.fori_loop(0, feats // wide, step, 0)

    def partial_of(t, u, h):
        if t == 0:
            each_t, own, every = h_t, y_own, y_all
        else:
            each_t, own, every = g_t, x_own, x_all
        if u == 0:
            forward(1 - t, own, every, h)
            forwarded(1 - t, every, h)
        return jnp.dot(each_t[u], every[h].reshape(GROUP * rows, chunk), preferred_element_type=F32)

    def z_copy(q, side, d):
        return remote(
            z_send.at[q, side, d - 1], z_got.at[q, side, d - 1], zs.at[q, side, d - 1], zr.at[q, side, d - 1],
            side_id[side],
        )

    def chain(t, u, between):
        q = 2 * t + u
        for d in range(steps - 1, 0, -1):
            if d == 1:
                between()
            for side in (0, 1):
                sends, behind = z_conditions(side, d)

                @pl.when(sends)
                def _():
                    partial[q] = partial_of(t, u, hi + d if side == 0 else hi - d)
                    if d < steps - 1:
                        @pl.when(behind)
                        def _():
                            z_copy(q, side, d + 1).wait_recv()
                            partial[q] = partial[q] + z_got[q, side, d].astype(F32)

                    z_send[q, side, d - 1] = partial[q].astype(BF16)
                    z_copy(q, side, d).start()

        partial[q] = partial_of(t, u, hi)

    def close(q):
        for side, behind in ((0, has_left), (1, has_right)):
            @pl.when(behind)
            def _():
                z_copy(q, side, 1).wait_recv()
                partial[q] = partial[q] + z_got[q, side, 0].astype(F32)

        return partial[q] * inv

    def arrived(t, u, every, every_t, copies):
        for cp in copies:
            cp.wait_recv()
        turn(u, every, every_t, (3,))

    rel_g = []

    def pass_on():
        for u in (0, 1):
            rel_g.append(relay(1, u, g_all, gat_g))
        spread(0, x_own, x_all, order)

    def nothing():
        pass

    arrived(0, 0, h_all, h_t, rel_h[0])
    chain(0, 0, nothing)
    lax.fori_loop(0, feats // wide, out_step, 0)
    own_out = to_owner(0, out_part, out_got)
    turn(1, h_all, h_t, (1, 2))
    for u in (0, 1):
        turn(u, g_all, g_t, (0,))
    for h in range(steps):
        x_all[h, 0] = x_own[lo, h]
    arrived(0, 1, h_all, h_t, rel_h[1])
    chain(0, 1, pass_on)
    lax.fori_loop(0, feats // wide, in_step, 0)
    own_in = to_owner(1, in_part, in_got)
    turn(0, g_all, g_t, (1, 2))
    arrived(1, 0, g_all, g_t, rel_g[0])
    chain(1, 0, nothing)
    turn(1, g_all, g_t, (1, 2))
    arrived(1, 1, g_all, g_t, rel_g[1])
    finish(out_part, out_got, x_raw, mixed_v, own_out)
    store_mixed = pltpu.make_async_copy(mixed_v, mixed_hbm, loc.at[4])
    store_mixed.start()
    chain(1, 1, nothing)
    finish(in_part, in_got, dy_raw, ing_v, own_in)
    store_ing = pltpu.make_async_copy(ing_v, ing_hbm, loc.at[5])
    store_ing.start()

    grad_v[0:wing] = close(0)
    grad_v[wing:] = close(1)
    store_down = pltpu.make_async_copy(grad_v, down_hbm, loc.at[6])
    store_down.start()
    up_v = pre.at[0:chunk, :]
    pre[0:chunk, 0:wing] = close(2).T
    pre[0:chunk, wing:] = close(3).T
    store_up = pltpu.make_async_copy(up_v, up_hbm, loc.at[7])
    store_up.start()

    for cp in sib_x + sib_y + own_out + own_in + sum(rel_h + rel_g, []):
        cp.wait_send()

    def drain(h, carry):
        for t, own, every in ((0, x_own, x_all), (1, y_own, y_all)):
            for o in mates:
                a2a_copy(t, own, every, o, h).wait_send()
                for k in sibs:
                    fwd_copy(t, every, o, h, k).wait_send()
        return carry

    lax.fori_loop(0, steps, drain, 0)
    for group in (gat_h, gat_g):
        for cp in group.values():
            cp.wait_send()
    for q in range(4):
        for d in range(steps - 1, 0, -1):
            for side in (0, 1):
                sends, _ = z_conditions(side, d)

                @pl.when(sends)
                def _():
                    z_copy(q, side, d).wait_send()
    for cp in (store_mixed, store_ing, store_down, store_up):
        cp.wait()


def hand_over(*refs):
    held, sems = refs[8:12], refs[12]
    parts = []
    for i in range(4):
        size = refs[i].shape[1] // 2
        parts += [(i, j, pl.ds(j * size, size)) for j in range(2)]
    reads = [pltpu.make_async_copy(refs[i].at[:, p], held[i].at[:, p], sems.at[0, i, j]) for i, j, p in parts]
    writes = [pltpu.make_async_copy(held[i].at[:, p], refs[4 + i].at[:, p], sems.at[1, i, j]) for i, j, p in parts]
    for cp in reads:
        cp.start()
    for get, put in zip(reads, writes):
        get.wait()
        put.start()
    for cp in writes:
        cp.wait()


def local(n_dp, n_blk, tokens, cotangent, w_up, w_down, active, width, counts):
    _, rows_own, feats = tokens.shape
    units = w_up.shape[2]
    rows = rows_own * n_blk
    chunk = feats // n_dp
    steps = n_dp // GROUP
    hops = max(steps - 1, 1)
    dma = pltpu.SemaphoreType.DMA
    anywhere = pl.BlockSpec(memory_space=pl.ANY)
    scalars = pl.BlockSpec(memory_space=pltpu.SMEM)
    scratch = [
        pltpu.VMEM((rows_own, feats), BF16),
        pltpu.VMEM((rows_own, feats), BF16),
        pltpu.VMEM((feats, units), BF16),
        pltpu.VMEM((units, feats), BF16),
        pltpu.VMEM((GROUP, steps, rows, chunk), BF16),
        pltpu.VMEM((GROUP, steps, rows, chunk), BF16),
        pltpu.VMEM((steps, GROUP, rows, chunk), BF16),
        pltpu.VMEM((steps, GROUP, rows, chunk), BF16),
        pltpu.VMEM((2, GROUP, rows, units // 2), BF16),
        pltpu.VMEM((2, GROUP, rows, units // 2), BF16),
        pltpu.VMEM((2, units // 2, GROUP * rows), BF16),
        pltpu.VMEM((2, units // 2, GROUP * rows), BF16),
        pltpu.VMEM((rows, units), F32),
        pltpu.VMEM((rows, units), F32),
        pltpu.VMEM((rows, feats), BF16),
        pltpu.VMEM((rows, feats), BF16),
        pltpu.VMEM((n_blk - 1, rows_own, feats), BF16),
        pltpu.VMEM((n_blk - 1, rows_own, feats), BF16),
        pltpu.VMEM((4, units // 2, chunk), F32),
        pltpu.VMEM((4, 2, hops, units // 2, chunk), BF16),
        pltpu.VMEM((4, 2, hops, units // 2, chunk), BF16),
        pltpu.VMEM((rows_own, feats), BF16),
        pltpu.VMEM((rows_own, feats), BF16),
        pltpu.VMEM((units, chunk), F32),
        dma((8,)),
        dma((2, n_blk)), dma((2, n_blk)),
        dma((2, GROUP, steps)), dma((2, GROUP, steps)),
        dma((2, GROUP, steps, n_blk)), dma((2, GROUP, steps, n_blk)),
        dma((2, 2, GROUP)), dma((2, 2, GROUP)),
        dma((2, 2, GROUP)), dma((2, 2, GROUP)),
        dma((2, n_blk)), dma((2, n_blk)),
        dma((4, 2, hops)), dma((4, 2, hops)),
    ]
    mixed, ing, up, down = pl.pallas_call(
        functools.partial(kernel, n_dp, n_blk),
        out_shape=(
            jax.ShapeDtypeStruct((rows_own, feats), BF16),
            jax.ShapeDtypeStruct((rows_own, feats), BF16),
            jax.ShapeDtypeStruct((chunk, units), F32),
            jax.ShapeDtypeStruct((units, chunk), F32),
        ),
        in_specs=[anywhere] * 4 + [scalars] * 3,
        out_specs=(anywhere,) * 4,
        scratch_shapes=scratch,
        compiler_params=pltpu.CompilerParams(
            collective_id=0, has_side_effects=True, vmem_limit_bytes=60 * 1024 * 1024
        ),
        cost_estimate=pl.CostEstimate(
            flops=12 * rows * feats * units, bytes_accessed=16 * 1024 * 1024, transcendentals=rows * units
        ),
    )(tokens[0], cotangent[0], w_up[0], w_down[0], active.T, width, counts)
    results = (mixed[None], ing[None], up[None], down[None])
    return pl.pallas_call(
        hand_over,
        out_shape=tuple(jax.ShapeDtypeStruct(r.shape, r.dtype) for r in results),
        in_specs=[anywhere] * 4,
        out_specs=(anywhere,) * 4,
        scratch_shapes=[pltpu.VMEM(r.shape, r.dtype) for r in results] + [dma((2, 4, 2))],
        compiler_params=pltpu.CompilerParams(vmem_limit_bytes=60 * 1024 * 1024),
    )(*results)


def solution(mesh):
    in_specs = (
        P("dp", "block", None),
        P("dp", "block", None),
        P("block", None, None),
        P("block", None, None),
        P(),
        P(),
        P(),
    )
    out_specs = (
        P("dp", "block", None),
        P("dp", "block", None),
        P("block", "dp", None),
        P("block", None, "dp"),
    )
    body = functools.partial(local, mesh.shape["dp"], mesh.shape["block"])
    return jax.shard_map(body, mesh=mesh, in_specs=in_specs, out_specs=out_specs, check_vma=False)
```
